32 devices in a mesh: groups: 2 (over x), blk: 16 (over z, y, core).
Axes of the slice: x: 2, y: 2, z: 4, core: 2. Of those that a mesh axis runs over, the one named last changes fastest.
Arguments:
- tokens: bfloat16 [256, 6144], P(('groups', 'blk')), parts along dimension 0, may hold values from -6 to 6
- norm_gain: float32 [6144], replicated, may hold values from 0.1 to 1.9
- w_expand: bfloat16 [6144, 24576], P(None, 'blk'), may hold values from -0.078125 to 0.078125
- b_expand: float32 [24576], P('blk'), may hold values from -3 to 3
- w_project: bfloat16 [24576, 6144], P('blk'), may hold values from -0.0390625 to 0.0390625
- b_project: float32 [6144], replicated, may hold values from -3 to 3
Outputs:
- mixed: bfloat16 [256, 6144], P(('groups', 'blk')), parts along dimension 0
The draws below stay inside these ranges and needn't reach their ends.
There are 2 independent parts, one for each index of `groups`. The reference program is written for one: setup_inputs(seed, part) draws one part's arguments, and reference() takes and returns one part's arrays. A program takes and returns all parts, laid end to end along the dimension named above; an argument that names none is the same for every part. Nothing has to cross between parts.
All inputs are finite; a program needn't handle non-finite values.
Results may differ from the reference program's by a relative error of at most 0.0055.
Values may be sent and summed in bfloat16 or wider, within the bound.
A program may use at most 128 MiB of HBM per device.

```python
import jax
import jax.numpy as jnp
from jax import lax

D = 6144
FF = 24576
TOKENS = 128


def steps_of(rng, dims, split, least, largest):
    def one(axis_at, blocks):
        steps = jax.random.uniform(jax.random.fold_in(jax.random.fold_in(rng, 6), axis_at), (blocks,), jnp.float32, least / len(split), largest / len(split))
        return jnp.repeat(jnp.exp(steps), dims[axis_at] // blocks).reshape((-1,) + (1,) * (len(dims) - axis_at - 1))

    loudness = one(*split[0])
    for cut in split[1:]:
        loudness = loudness * one(*cut)
    return loudness


def gaussian(rng, shape, scale, most, cuts=(), held_as=jnp.bfloat16):
    drawn = jax.random.normal(rng, shape, jnp.float32) * scale
    if len(cuts) > 0:
        drawn = steps_of(rng, shape, cuts, -0.22, 0.18) * drawn
    return jnp.clip(drawn, min=-most, max=most).astype(held_as)


def setup_inputs(seed: int = 0, part: int = 0) -> dict:
    key_of = jax.random.split(jax.random.key(seed), 7)
    own_keys = jax.random.split(jax.random.fold_in(key_of[6], part), 7)
    return {
        "tokens": gaussian(own_keys[0], (TOKENS, D), 1.0, 6.0, ((0, 16),)),
        "norm_gain": jnp.clip(1.0 + 0.18 * jax.random.normal(key_of[1], (D,), jnp.float32), 0.1, 1.9),
        "w_expand": gaussian(key_of[2], (D, FF), D ** -0.5, 0.078125, ((1, 16),)),
        "b_expand": gaussian(key_of[3], (FF,), 0.5, 3.0, ((0, 16),), jnp.float32),
        "w_project": gaussian(key_of[4], (FF, D), FF ** -0.5, 0.0390625, ((0, 16),)),
        "b_project": gaussian(key_of[5], (D,), 0.5, 3.0, (), jnp.float32),
    }


def gelu_tanh(value):
    return 0.5 * value * (1.0 + jnp.tanh(0.7978845608 * (value + 0.044715 * value * value * value)))

def reference(tokens, norm_gain, w_expand, b_expand, w_project, b_project):
    wide = tokens.astype(jnp.float32)
    row_mean = lax.optimization_barrier(jnp.mean(wide, axis=1, keepdims=True))
    centred = wide - row_mean
    row_spread = lax.optimization_barrier(jnp.mean(centred * centred, axis=1, keepdims=True))
    normed = (centred / jnp.sqrt(row_spread + 1e-06) * norm_gain).astype(jnp.bfloat16)
    hidden = gelu_tanh(jnp.dot(normed, w_expand, preferred_element_type=jnp.float32) + b_expand).astype(jnp.bfloat16)
    mixed = jnp.dot(hidden, w_project, preferred_element_type=jnp.float32) + b_project
    return mixed.astype(jnp.bfloat16)
```

```python
import functools

import jax
import jax.numpy as jnp
from jax import lax
from jax.experimental import pallas as pl
from jax.experimental.pallas import tpu as pltpu
from jax.sharding import PartitionSpec as P

F32, BF16 = jnp.float32, jnp.bfloat16
CHUNKS = 2


def gelu_tanh(value):
    return 0.5 * value * (1.0 + jnp.tanh(0.7978845608 * (value + 0.044715 * value * value * value)))


def tile_of(size, most=512):
    return max(t for t in range(128, most + 1, 128) if size % t == 0)


def chip_at(place, chips):
    if chips > 8:
        return place
    half = chips // 2
    down = lax.div(place, half)
    return (1 - down) * 2 * place + down * (2 * (chips - 1 - place) + 1)


def place_of(chip, chips):
    if chips > 8:
        return chip
    high, low = lax.div(chip, 2), lax.rem(chip, 2)
    return (1 - low) * high + low * (chips - 1 - high)


def kernel(
    n, wire, tok, gain, b1, b2, w1, w2, out,
    w1v, w2v, swap, xbuf, hid, snd, sib_in, own, ring_in, ring_out, fin, fin_in,
    w1_sem, w2_sem, swap_sem, ag_send, ag_recv, fw_send, fw_recv, sib_send, sib_recv, rs_send, rs_recv, fin_send, fin_recv,
):
    rows, width = tok.shape
    pair = 2 * rows
    chips = n // 2
    parts = 2 * CHUNKS
    wide = width // parts
    tokens = rows * n
    units = w1.shape[1]

    me = lax.axis_index("blk")
    core, chip = lax.rem(me, 2), lax.div(me, 2)
    place = place_of(chip, chips)
    step_by = 1 - 2 * core

    def around(k):
        return chip_at(lax.rem(place + step_by * k + 2 * chips, chips), chips)

    following, previous = around(1) * 2 + core, around(-1) * 2 + core
    sibling = chip * 2 + 1 - core

    def send(src, dst, send_sem, recv_sem, to):
        return pltpu.make_async_remote_copy(
            src_ref=src, dst_ref=dst, send_sem=send_sem, recv_sem=recv_sem,
            device_id={"blk": to}, device_id_type=pl.DeviceIdType.MESH,
        )

    barrier = pltpu.get_barrier_semaphore()
    for other in (following, previous, sibling):
        pl.semaphore_signal(barrier, inc=1, device_id={"blk": other}, device_id_type=pl.DeviceIdType.MESH)

    def w1_copy(g):
        at = pl.ds(g * wide, wide)
        return pltpu.make_async_copy(w1.at[at], w1v.at[at], w1_sem.at[g])

    def w2_copy(k):
        j, mine = k % CHUNKS, k // CHUNKS
        g = (core if mine else 1 - core) * CHUNKS + j
        at = pl.ds(pl.multiple_of(g * wide, wide), wide)
        return pltpu.make_async_copy(w2.at[:, at], w2v.at[:, at], w2_sem.at[k])

    for g in range(parts):
        w1_copy(g).start()
    for k in range(parts):
        w2_copy(k).start()

    x = tok[...].astype(F32)
    mean = jnp.mean(x, axis=1, keepdims=True)
    centred = x - mean
    spread = jnp.mean(centred * centred, axis=1, keepdims=True)
    normed = (centred / jnp.sqrt(spread + 1e-06) * gain[...]).astype(BF16).astype(F32)
    swap[core] = normed

    pl.semaphore_wait(barrier, 3)
    swapped = send(swap.at[core], swap.at[core], swap_sem.at[0], swap_sem.at[1], sibling)
    swapped.start()
    send(swap.at[1 - core], swap.at[1 - core], swap_sem.at[0], swap_sem.at[1], sibling).wait_recv()

    def rows_of(where):
        return pl.ds(pl.multiple_of(where * pair, pair), pair)

    both = jnp.concatenate([swap[0], swap[1]], axis=0).astype(BF16)
    for g in range(parts):
        xbuf[g, rows_of(chip), :] = both[:, g * wide:(g + 1) * wide]

    def ag(s, j, where, to, send_sem, recv_sem, half):
        block = xbuf.at[half * CHUNKS + j, rows_of(where)]
        return send(block, block, send_sem.at[s, j], recv_sem.at[s, j], to)

    for j in range(CHUNKS):
        ag(0, j, chip, following, ag_send, ag_recv, core).start()

    @pl.loop(1, chips)
    def _(s):
        where = around(-s)
        for j in range(CHUNKS):
            ag(s - 1, j, where, following, ag_send, ag_recv, core).wait_recv()

            @pl.when(s < chips - 1)
            def _():
                ag(s, j, where, following, ag_send, ag_recv, core).start()

            ag(s - 1, j, where, sibling, fw_send, fw_recv, core).start()

    for g in range(parts):
        w1_copy(g).wait()

    @pl.loop(1, chips)
    def _(s):
        for j in range(CHUNKS):
            ag(s - 1, j, around(s), sibling, fw_send, fw_recv, 1 - core).wait_recv()

    tile = tile_of(units)

    @pl.loop(0, units // tile)
    def _(t):
        at = pl.ds(pl.multiple_of(t * tile, tile), tile)
        total = jnp.dot(xbuf[0], w1v[0:wide, at], preferred_element_type=F32)
        for g in range(1, parts):
            total += jnp.dot(xbuf[g], w1v[g * wide:(g + 1) * wide, at], preferred_element_type=F32)
        hid[:, at] = gelu_tanh(total + b1[:, at]).astype(BF16)

    cut = tile_of(wide)

    def project(half, j, store):
        @pl.loop(0, wide // cut)
        def _(t):
            at = pl.ds(pl.multiple_of(t * cut, cut), cut)
            start = (half * CHUNKS + j) * wide + t * cut
            cols = pl.ds(pl.multiple_of(start, cut), cut)
            store(at, jnp.dot(hid[...], w2v[:, cols], preferred_element_type=F32))

    def sib_copy(j):
        return send(snd.at[j], sib_in.at[j], sib_send.at[j], sib_recv.at[j], sibling)

    for j in range(CHUNKS):
        w2_copy(j).wait()

        def keep_theirs(at, value, j=j):
            snd[j, :, at] = value.astype(wire)

        project(1 - core, j, keep_theirs)
        sib_copy(j).start()

    def rs_copy(s, j):
        return send(ring_out.at[s, j], ring_in.at[s, j], rs_send.at[s, j], rs_recv.at[s, j], following)

    def ours(j, where):
        return own[j, rows_of(where), :] + sib_in[j, rows_of(where), :].astype(F32)

    for j in range(CHUNKS):
        w2_copy(CHUNKS + j).wait()

        def keep_own(at, value, j=j):
            own[j, :, at] = value

        project(core, j, keep_own)
        sib_copy(j).wait_recv()
        ring_out[0, j] = ours(j, around(-1)).astype(wire)
        rs_copy(0, j).start()

    @pl.loop(1, chips - 1)
    def _(s):
        where = around(-s - 1)
        for j in range(CHUNKS):
            rs_copy(s - 1, j).wait_recv()
            ring_out[s, j] = (ours(j, where) + ring_in[s - 1, j].astype(F32)).astype(wire)
            rs_copy(s, j).start()

    def fin_copy(j):
        return send(fin.at[j, 1 - core], fin_in.at[j], fin_send.at[j], fin_recv.at[j], sibling)

    for j in range(CHUNKS):
        rs_copy(chips - 2, j).wait_recv()
        total = ours(j, chip) + ring_in[chips - 2, j].astype(F32)
        fin[j, 0] = total[:rows]
        fin[j, 1] = total[rows:]
        fin_copy(j).start()
    for j in range(CHUNKS):
        fin_copy(j).wait_recv()
    for g in range(parts):
        at = slice(g * wide, (g + 1) * wide)
        j = g % CHUNKS
        total = jnp.where(core == g // CHUNKS, fin[j, core], fin_in[j])
        out[:, at] = (total + b2[:, at]).astype(BF16)

    swapped.wait_send()
    for j in range(CHUNKS):
        sib_copy(j).wait_send()
        fin_copy(j).wait_send()

    @pl.loop(0, chips - 1)
    def _(s):
        for j in range(CHUNKS):
            ag(s, j, chip, following, ag_send, ag_recv, core).wait_send()
            ag(s, j, chip, sibling, fw_send, fw_recv, core).wait_send()
            rs_copy(s, j).wait_send()


def on_device(n, tokens, norm_gain, w_expand, b_expand, w_project, b_project):
    rows, width = tokens.shape
    units = w_expand.shape[1]
    chips = n // 2
    pair, total = 2 * rows, rows * n
    wide = width // (2 * CHUNKS)
    wire = BF16 if chips <= 8 else F32
    dma = pltpu.SemaphoreType.DMA
    vmem = pl.BlockSpec(memory_space=pltpu.VMEM)
    hbm = pl.BlockSpec(memory_space=pl.ANY)
    return pl.pallas_call(
        functools.partial(kernel, n, wire),
        out_shape=jax.ShapeDtypeStruct((rows, width), BF16),
        in_specs=[vmem] * 4 + [hbm] * 2,
        out_specs=vmem,
        scratch_shapes=[
            pltpu.VMEM((width, units), BF16),
            pltpu.VMEM((units, width), BF16),
            pltpu.VMEM((2, rows, width), F32),
            pltpu.VMEM((2 * CHUNKS, total, wide), BF16),
            pltpu.VMEM((total, units), BF16),
            pltpu.VMEM((CHUNKS, total, wide), wire),
            pltpu.VMEM((CHUNKS, total, wide), wire),
            pltpu.VMEM((CHUNKS, total, wide), F32),
            pltpu.VMEM((chips - 1, CHUNKS, pair, wide), wire),
            pltpu.VMEM((chips - 1, CHUNKS, pair, wide), wire),
            pltpu.VMEM((CHUNKS, 2, rows, wide), F32),
            pltpu.VMEM((CHUNKS, rows, wide), F32),
            dma((2 * CHUNKS,)),
            dma((2 * CHUNKS,)),
            dma((2,)),
            dma((chips - 1, CHUNKS)),
            dma((chips - 1, CHUNKS)),
            dma((chips - 1, CHUNKS)),
            dma((chips - 1, CHUNKS)),
            dma((CHUNKS,)),
            dma((CHUNKS,)),
            dma((chips - 1, CHUNKS)),
            dma((chips - 1, CHUNKS)),
            dma((CHUNKS,)),
            dma((CHUNKS,)),
        ],
        compiler_params=pltpu.CompilerParams(
            collective_id=0, has_side_effects=True, vmem_limit_bytes=60 * 1024 * 1024
        ),
    )(tokens, norm_gain[None], b_expand[None], b_project[None], w_expand, w_project)


def solution(mesh):
    placed = (P(("groups", "blk"), None), P(), P(None, "blk"), P("blk"), P("blk", None), P())
    return jax.shard_map(
        functools.partial(on_device, mesh.shape["blk"]),
        mesh=mesh, in_specs=placed, out_specs=P(("groups", "blk"), None), check_vma=False,
    )
```

```python
import functools

import jax
import jax.numpy as jnp
from jax import lax
from jax.experimental import pallas as pl
from jax.experimental.pallas import tpu as pltpu
from jax.sharding import PartitionSpec as P

F32, BF16 = jnp.float32, jnp.bfloat16
CHUNKS = 2


def gelu_tanh(value):
    return 0.5 * value * (1.0 + jnp.tanh(0.7978845608 * (value + 0.044715 * value * value * value)))


def tile_of(size, most=768):
    step = 256 if size % 256 == 0 else 128
    return max(t for t in range(step, most + 1, step) if size % t == 0)


def chip_at(place, chips):
    if chips > 8:
        return place
    half = chips // 2
    down = lax.div(place, half)
    return (1 - down) * 2 * place + down * (2 * (chips - 1 - place) + 1)


def place_of(chip, chips):
    if chips > 8:
        return chip
    high, low = lax.div(chip, 2), lax.rem(chip, 2)
    return (1 - low) * high + low * (chips - 1 - high)


def kernel(
    n, tok, gain, b1, b2, w1, w2, out,
    w1v, w2v, xin, lhs, hid, snd, sib_in, own, ring_in, ring_out, fin, fin_in,
    w1_sem, w2_sem, ag_send, ag_recv, fw_send, fw_recv, sib_send, sib_recv, rs_send, rs_recv, fin_send, fin_recv,
):
    rows, width = tok.shape
    pair = 2 * rows
    chips = n // 2
    far = chips // 2
    half = width // 2
    wide = half // CHUNKS
    units = w1.shape[1]
    wire = ring_in.dtype
    ways = (0, 1)

    me = lax.axis_index("blk")
    core, chip = lax.rem(me, 2), lax.div(me, 2)
    place = place_of(chip, chips)

    def around(k):
        return chip_at(lax.rem(place + k + 2 * chips, chips), chips)

    sign = (1, -1)
    ahead = [around(sign[w]) * 2 + core for w in ways]
    sibling = chip * 2 + 1 - core

    def takes(way, j):
        return (j % 2) == way

    def send(src, dst, send_sem, recv_sem, to):
        return pltpu.make_async_remote_copy(
            src_ref=src, dst_ref=dst, send_sem=send_sem, recv_sem=recv_sem,
            device_id={"blk": to}, device_id_type=pl.DeviceIdType.MESH,
        )

    barrier = pltpu.get_barrier_semaphore()
    for other in (*ahead, sibling):
        pl.semaphore_signal(barrier, inc=1, device_id={"blk": other}, device_id_type=pl.DeviceIdType.MESH)

    def w1_copy(h):
        at = pl.ds(h * half, half)
        return pltpu.make_async_copy(w1.at[at], w1v.at[at], w1_sem.at[h])

    def w2_copy(h):
        at = pl.ds(pl.multiple_of((core if h else 1 - core) * half, half), half)
        return pltpu.make_async_copy(w2.at[:, at], w2v.at[:, at], w2_sem.at[h])

    for h in ways:
        w1_copy(h).start()
    for h in ways:
        w2_copy(h).start()

    x = tok[...].astype(F32)
    mean = jnp.mean(x, axis=1, keepdims=True)
    centred = x - mean
    spread = jnp.mean(centred * centred, axis=1, keepdims=True)
    normed = centred / jnp.sqrt(spread + 1e-06) * gain[...]
    folded = jnp.concatenate([normed[:, :half], normed[:, half:]], axis=0).astype(BF16)
    for j in range(CHUNKS):
        xin[me, j] = folded[:, j * wide:(j + 1) * wide]

    pl.semaphore_wait(barrier, 3)

    def ag(way, s, j, where):
        block = xin.at[where * 2 + core, j]
        return send(block, block, ag_send.at[way, s, j], ag_recv.at[way, s, j], ahead[way])

    def fw(way, s, j, where, side):
        block = xin.at[where * 2 + side, j]
        return send(block, block, fw_send.at[way, s, j], fw_recv.at[way, s, j], sibling)

    def rows_of(where):
        return pl.ds(pl.multiple_of(where * pair, pair), pair)

    def assemble(where, chunks):
        for j in chunks:
            first, second = xin[where * 2, j].astype(F32), xin[where * 2 + 1, j].astype(F32)
            at = slice(j * wide, (j + 1) * wide)
            lhs[0, rows_of(where), at] = jnp.concatenate([first[:rows], second[:rows]], axis=0).astype(BF16)
            lhs[1, rows_of(where), at] = jnp.concatenate([first[rows:], second[rows:]], axis=0).astype(BF16)

    every = range(CHUNKS)
    for j in every:
        for way in ways:
            ag(way, 0, j, chip).start()
    for j in every:
        fw(0, 0, j, chip, core).start()

    def gather(s, last, next_last):
        for j in every:
            for way in ways:
                if last and not takes(way, j):
                    continue
                where = around(-sign[way] * s)
                ag(way, s - 1, j, where).wait_recv()
                if not last and (not next_last or takes(way, j)):
                    ag(way, s, j, where).start()
                fw(way, s, j, where, core).start()

    def take(s, last):
        for way in ways:
            where = around(-sign[way] * s)
            chunks = [j for j in every if not last or takes(way, j)]
            for j in chunks:
                fw(way, s, j, where, 1 - core).wait_recv()
            assemble(where, chunks)

    gather(1, False, far == 2)
    for j in every:
        fw(0, 0, j, chip, 1 - core).wait_recv()
    assemble(chip, every)

    @pl.loop(2, far - 1)
    def _(s):
        gather(s, False, False)
        take(s - 1, False)

    if far > 2:
        gather(far - 1, False, True)
        take(far - 2, False)
    gather(far, True, False)
    take(far - 1, False)
    take(far, True)

    for h in ways:
        w1_copy(h).wait()

    tile = tile_of(units)

    @pl.loop(0, units // tile)
    def _(t):
        at = pl.ds(pl.multiple_of(t * tile, tile), tile)
        total = jnp.dot(lhs[0], w1v[:half, at], preferred_element_type=F32)
        total += jnp.dot(lhs[1], w1v[half:, at], preferred_element_type=F32)
        hid[:, at] = gelu_tanh(total + b1[:, at]).astype(BF16)

    cut = tile_of(wide)

    def project(side, j, store):
        @pl.loop(0, wide // cut)
        def _(t):
            at = pl.ds(pl.multiple_of(t * cut, cut), cut)
            cols = pl.ds(pl.multiple_of(side * half + j * wide + t * cut, cut), cut)
            store(at, jnp.dot(hid[...], w2v[:, cols], preferred_element_type=F32))

    def sib_copy(j):
        return send(snd.at[j], sib_in.at[j], sib_send.at[j], sib_recv.at[j], sibling)

    w2_copy(0).wait()
    for j in every:

        def keep_theirs(at, value, j=j):
            snd[j, :, at] = value.astype(BF16)

        project(1 - core, j, keep_theirs)
        sib_copy(j).start()

    def rs(way, k, j):
        return send(
            ring_out.at[way, k - 1, j], ring_in.at[way, k - 1, j],
            rs_send.at[way, k - 1, j], rs_recv.at[way, k - 1, j], ahead[way],
        )

    def ours(j, where):
        return own[j, rows_of(where), :] + sib_in[j, rows_of(where), :].astype(F32)

    def pass_on(way, k, j, more):
        total = ours(j, around(sign[way] * k))
        if more:
            rs(way, k + 1, j).wait_recv()
            total += ring_in[way, k, j].astype(F32)
        ring_out[way, k - 1, j] = total.astype(wire)
        rs(way, k, j).start()

    w2_copy(1).wait()
    for j in every:

        def keep_own(at, value, j=j):
            own[j, :, at] = value

        project(core, j, keep_own)
        sib_copy(j).wait_recv()
        for way in ways:
            if takes(way, j):
                pass_on(way, far, j, False)
        for way in ways:
            if not takes(way, j):
                pass_on(way, far - 1, j, False)

    for j in every:
        for way in ways:
            if takes(way, j):
                pass_on(way, far - 1, j, True)

    @pl.loop(2, far)
    def _(s):
        for j in every:
            for way in ways:
                pass_on(way, far - s, j, True)

    def fin_copy(j):
        return send(fin.at[j, 1 - core], fin_in.at[j], fin_send.at[j], fin_recv.at[j], sibling)

    for j in every:
        total = ours(j, chip)
        for way in ways:
            rs(way, 1, j).wait_recv()
            total += ring_in[way, 0, j].astype(F32)
        fin[j, 0] = total[:rows]
        fin[j, 1] = total[rows:]
        fin_copy(j).start()
    for j in every:
        fin_copy(j).wait_recv()
    for g in range(2 * CHUNKS):
        at = slice(g * wide, (g + 1) * wide)
        j = g % CHUNKS
        total = jnp.where(core == g // CHUNKS, fin[j, core], fin_in[j])
        out[:, at] = (total + b2[:, at]).astype(BF16)

    def sent(s, last):
        for j in every:
            for way in ways:
                if not last or takes(way, j):
                    ag(way, s - 1, j, chip).wait_send()
                    fw(way, s, j, chip, core).wait_send()
                    rs(way, s, j).wait_send()

    for j in every:
        fw(0, 0, j, chip, core).wait_send()
        sib_copy(j).wait_send()
        fin_copy(j).wait_send()

    @pl.loop(1, far)
    def _(s):
        sent(s, False)

    sent(far, True)


def on_device(n, tokens, norm_gain, w_expand, b_expand, w_project, b_project):
    rows, width = tokens.shape
    units = w_expand.shape[1]
    chips = n // 2
    far = chips // 2
    pair, total = 2 * rows, rows * n
    half = width // 2
    wide = half // CHUNKS
    wire = BF16 if chips <= 8 else F32
    dma = pltpu.SemaphoreType.DMA
    vmem = pl.BlockSpec(memory_space=pltpu.VMEM)
    hbm = pl.BlockSpec(memory_space=pl.ANY)
    return pl.pallas_call(
        functools.partial(kernel, n),
        out_shape=jax.ShapeDtypeStruct((rows, width), BF16),
        in_specs=[vmem] * 4 + [hbm] * 2,
        out_specs=vmem,
        scratch_shapes=[
            pltpu.VMEM((width, units), BF16),
            pltpu.VMEM((units, width), BF16),
            pltpu.VMEM((n, CHUNKS, pair, wide), BF16),
            pltpu.VMEM((2, total, half), BF16),
            pltpu.VMEM((total, units), BF16),
            pltpu.VMEM((CHUNKS, total, wide), BF16),
            pltpu.VMEM((CHUNKS, total, wide), BF16),
            pltpu.VMEM((CHUNKS, total, wide), F32),
            pltpu.VMEM((2, far, CHUNKS, pair, wide), wire),
            pltpu.VMEM((2, far, CHUNKS, pair, wide), wire),
            pltpu.VMEM((CHUNKS, 2, rows, wide), F32),
            pltpu.VMEM((CHUNKS, rows, wide), F32),
            dma((2,)),
            dma((2,)),
            dma((2, far, CHUNKS)),
            dma((2, far, CHUNKS)),
            dma((2, far + 1, CHUNKS)),
            dma((2, far + 1, CHUNKS)),
            dma((CHUNKS,)),
            dma((CHUNKS,)),
            dma((2, far, CHUNKS)),
            dma((2, far, CHUNKS)),
            dma((CHUNKS,)),
            dma((CHUNKS,)),
        ],
        compiler_params=pltpu.CompilerParams(
            collective_id=0, has_side_effects=True, vmem_limit_bytes=60 * 1024 * 1024
        ),
    )(tokens, norm_gain[None], b_expand[None], b_project[None], w_expand, w_project)


def solution(mesh):
    placed = (P(("groups", "blk"), None), P(), P(None, "blk"), P("blk"), P("blk", None), P())
    return jax.shard_map(
        functools.partial(on_device, mesh.shape["blk"]),
        mesh=mesh, in_specs=placed, out_specs=P(("groups", "blk"), None), check_vma=False,
    )
```

```python
import functools

import jax
import jax.numpy as jnp
from jax import lax
from jax.experimental import pallas as pl
from jax.experimental.pallas import tpu as pltpu
from jax.sharding import PartitionSpec as P

F32, BF16 = jnp.float32, jnp.bfloat16
CHUNKS = 2


def gelu_tanh(value):
    return 0.5 * value * (1.0 + jnp.tanh(0.7978845608 * (value + 0.044715 * value * value * value)))


def tile_of(size, most=768):
    step = 256 if size % 256 == 0 else 128
    return max(t for t in range(step, most + 1, step) if size % t == 0)


def chip_at(place, chips):
    if chips > 8:
        return place
    half = chips // 2
    down = lax.div(place, half)
    return (1 - down) * 2 * place + down * (2 * (chips - 1 - place) + 1)


def place_of(chip, chips):
    if chips > 8:
        return chip
    high, low = lax.div(chip, 2), lax.rem(chip, 2)
    return (1 - low) * high + low * (chips - 1 - high)


def kernel(
    n, tok, gain, b1, b2, w1, w2, out,
    w1v, w2v, xin, lhs, hid, snd, sib_in, own, ring_in, ring_out, last_in, last_out, ext_in,
    w1_sem, w2_sem, ag_send, ag_recv, fw_send, fw_recv, sib_send, sib_recv, rs_send, rs_recv, last_send, last_recv, ext_send, ext_recv,
):
    rows, width = tok.shape
    pair = 2 * rows
    chips = n // 2
    far = chips // 2
    half = width // 2
    wide = half // CHUNKS
    units = w1.shape[1]
    wire = ring_in.dtype
    ways = (0, 1)

    me = lax.axis_index("blk")
    core, chip = lax.rem(me, 2), lax.div(me, 2)
    place = place_of(chip, chips)

    def around(k):
        return chip_at(lax.rem(place + k + 2 * chips, chips), chips)

    sign = (1, -1)
    ahead = [around(sign[w]) * 2 + core for w in ways]
    beyond = [around(2 * sign[w]) * 2 + core for w in ways]
    across = [around(sign[w]) * 2 + 1 - core for w in ways]
    sibling = chip * 2 + 1 - core

    def takes(way, j):
        return (j % 2) == way

    def send(src, dst, send_sem, recv_sem, to):
        return pltpu.make_async_remote_copy(
            src_ref=src, dst_ref=dst, send_sem=send_sem, recv_sem=recv_sem,
            device_id={"blk": to}, device_id_type=pl.DeviceIdType.MESH,
        )

    barrier = pltpu.get_barrier_semaphore()
    for other in (*ahead, *across, *beyond, sibling):
        pl.semaphore_signal(barrier, inc=1, device_id={"blk": other}, device_id_type=pl.DeviceIdType.MESH)

    def w1_copy(h):
        at = pl.ds(h * half, half)
        return pltpu.make_async_copy(w1.at[at], w1v.at[at], w1_sem.at[h])

    def w2_copy(h):
        at = pl.ds(pl.multiple_of((core if h else 1 - core) * half, half), half)
        return pltpu.make_async_copy(w2.at[:, at], w2v.at[:, at], w2_sem.at[h])

    for h in ways:
        w1_copy(h).start()
    for h in ways:
        w2_copy(h).start()

    x = tok[...].astype(F32)
    mean = jnp.mean(x, axis=1, keepdims=True)
    centred = x - mean
    spread = jnp.mean(centred * centred, axis=1, keepdims=True)
    normed = centred / jnp.sqrt(spread + 1e-06) * gain[...]
    folded = jnp.concatenate([normed[:, :half], normed[:, half:]], axis=0).astype(BF16)
    for j in range(CHUNKS):
        xin[me, j] = folded[:, j * wide:(j + 1) * wide]

    pl.semaphore_wait(barrier, 7)

    def ag(way, s, j, where, leap=False):
        block = xin.at[where * 2 + core, j]
        return send(block, block, ag_send.at[way, s, j], ag_recv.at[way, s, j], (beyond if leap else ahead)[way])

    def fw(way, s, j, where, side):
        block = xin.at[where * 2 + side, j]
        return send(block, block, fw_send.at[way, s, j], fw_recv.at[way, s, j], sibling)

    def rows_of(where):
        return pl.ds(pl.multiple_of(where * pair, pair), pair)

    def assemble(where, chunks):
        for j in chunks:
            first, second = xin[where * 2, j].astype(F32), xin[where * 2 + 1, j].astype(F32)
            at = slice(j * wide, (j + 1) * wide)
            lhs[0, rows_of(where), at] = jnp.concatenate([first[:rows], second[:rows]], axis=0).astype(BF16)
            lhs[1, rows_of(where), at] = jnp.concatenate([first[rows:], second[rows:]], axis=0).astype(BF16)

    every = range(CHUNKS)
    for j in every:
        for way in ways:
            ag(way, 0, j, chip).start()
    for j in every:
        fw(0, 0, j, chip, core).start()

    def gather(s, onward, leap, last=False):
        for j in every:
            for way in ways:
                if last and not takes(way, j):
                    continue
                where = around(-sign[way] * s)
                ag(way, s - 1, j, where).wait_recv()
                if leap and takes(way, j):
                    ag(way, s + 1, j, where, True).start()
                if onward:
                    ag(way, s, j, where).start()
                fw(way, s, j, where, core).start()

    def take(s, last):
        for way in ways:
            where = around(-sign[way] * s)
            chunks = [j for j in every if not last or takes(way, j)]
            for j in chunks:
                fw(way, s, j, where, 1 - core).wait_recv()
            assemble(where, chunks)

    gather(1, True, False)
    for j in every:
        fw(0, 0, j, chip, 1 - core).wait_recv()
    assemble(chip, every)

    @pl.loop(2, far - 2)
    def _(s):
        gather(s, True, False)
        take(s - 1, False)

    gather(far - 2, True, True)
    take(far - 3, False)
    gather(far - 1, False, False)
    gather(far, False, False, True)
    take(far - 2, False)
    take(far - 1, False)
    take(far, True)

    for h in ways:
        w1_copy(h).wait()

    tile = tile_of(units)

    @pl.loop(0, units // tile)
    def _(t):
        at = pl.ds(pl.multiple_of(t * tile, tile), tile)
        total = jnp.dot(lhs[0], w1v[:half, at], preferred_element_type=F32)
        total += jnp.dot(lhs[1], w1v[half:, at], preferred_element_type=F32)
        hid[:, at] = gelu_tanh(total + b1[:, at]).astype(BF16)

    cut = tile_of(wide)

    def project(side, j, store):
        @pl.loop(0, wide // cut)
        def _(t):
            at = pl.ds(pl.multiple_of(t * cut, cut), cut)
            cols = pl.ds(pl.multiple_of(side * half + j * wide + t * cut, cut), cut)
            store(at, jnp.dot(hid[...], w2v[:, cols], preferred_element_type=F32))

    def sib_copy(j):
        return send(snd.at[j], sib_in.at[j], sib_send.at[j], sib_recv.at[j], sibling)

    w2_copy(0).wait()
    for j in every:

        def keep_theirs(at, value, j=j):
            snd[j, :, at] = value.astype(BF16)

        project(1 - core, j, keep_theirs)
        sib_copy(j).start()

    def rs(way, k, j, leap=False):
        return send(
            ring_out.at[way, k - 1, j], ring_in.at[way, k - 1, j],
            rs_send.at[way, k - 1, j], rs_recv.at[way, k - 1, j], (beyond if leap else ahead)[way],
        )

    def ours(j, where):
        return own[j, rows_of(where), :] + sib_in[j, rows_of(where), :].astype(F32)

    def came(way, k, j):
        rs(way, k, j).wait_recv()
        return ring_in[way, k - 1, j].astype(F32)

    def running(way, k, j):
        total = ours(j, around(sign[way] * k))
        if isinstance(k, int) and k >= far - 1:
            return total
        total += came(way, k + 1, j)
        if isinstance(k, int) and k == far - 2 and takes(way, j):
            total += came(way, k + 2, j)
        return total

    def pass_on(way, k, j, leap=False):
        ring_out[way, k - 1, j] = running(way, k, j).astype(wire)
        rs(way, k, j, leap).start()

    def last_copy(way, j, side):
        to = around(sign[way]) * 2 + side
        return send(
            last_out.at[way, side, j], last_in.at[way, core, j],
            last_send.at[way, side, j], last_recv.at[way, core, j], to,
        )

    def last_came(way, j, side):
        return send(
            last_out.at[way, 0, j], last_in.at[way, side, j],
            last_send.at[way, 0, j], last_recv.at[way, side, j], sibling,
        )

    def fold(value):
        return jnp.concatenate([value[:, :wide // 2], value[:, wide // 2:]], axis=0)

    def unfold(value):
        return jnp.concatenate([value[:rows], value[rows:]], axis=1)

    def ext_copy(j):
        theirs = pl.ds(pl.multiple_of(chip * pair + (1 - core) * rows, rows), rows)
        return send(own.at[j, theirs], ext_in.at[j], ext_send.at[j], ext_recv.at[j], sibling)

    w2_copy(1).wait()
    for j in every:

        def keep_own(at, value, j=j):
            own[j, :, at] = value

        project(core, j, keep_own)
        sib_copy(j).wait_recv()
        for way in ways:
            if takes(way, j):
                pass_on(way, far, j, True)
        for way in ways:
            pass_on(way, far - 1, j)
        ext_copy(j).start()

    if far > 3:
        for j in every:
            for way in ways:
                pass_on(way, far - 2, j)

    @pl.loop(3, far - 1)
    def _(s):
        for j in every:
            for way in ways:
                pass_on(way, far - s, j)

    for j in every:
        for way in ways:
            total = running(way, 1, j)
            for side in (0, 1):
                last_out[way, side, j] = fold(total[side * rows:(side + 1) * rows]).astype(wire)
                last_copy(way, j, side).start()

    def my_rows(value):
        return jnp.where(core == 0, value[:rows], value[rows:])

    for j in every:
        ext_copy(j).wait_recv()
        mine = own[j, pl.ds(pl.multiple_of(chip * pair + core * rows, rows), rows), :]
        mine += my_rows(sib_in[j, rows_of(chip), :].astype(F32))
        other = my_rows(snd[j, rows_of(chip), :].astype(F32)) + ext_in[j]
        for side in (0, 1):
            start = side * half + j * wide
            at = slice(start, start + wide)
            total = jnp.where(core == side, mine, other) + b2[:, at]
            for way in ways:
                last_came(way, j, side).wait_recv()
                total += unfold(last_in[way, side, j].astype(F32))
            out[:, at] = total.astype(BF16)

    def sent(s, last):
        for j in every:
            for way in ways:
                if not last or takes(way, j):
                    ag(way, s - 1, j, chip).wait_send()
                    fw(way, s, j, chip, core).wait_send()

    def scattered(k, last):
        for j in every:
            for way in ways:
                if not last or takes(way, j):
                    rs(way, k, j).wait_send()

    for j in every:
        fw(0, 0, j, chip, core).wait_send()
        sib_copy(j).wait_send()
        ext_copy(j).wait_send()
        for way in ways:
            for side in (0, 1):
                last_copy(way, j, side).wait_send()

    @pl.loop(1, far)
    def _(s):
        sent(s, False)

    @pl.loop(2, far)
    def _(k):
        scattered(k, False)

    sent(far, True)
    scattered(far, True)


def on_device(n, tokens, norm_gain, w_expand, b_expand, w_project, b_project):
    rows, width = tokens.shape
    units = w_expand.shape[1]
    chips = n // 2
    far = chips // 2
    pair, total = 2 * rows, rows * n
    half = width // 2
    wide = half // CHUNKS
    wire = BF16 if chips <= 8 else F32
    dma = pltpu.SemaphoreType.DMA
    vmem = pl.BlockSpec(memory_space=pltpu.VMEM)
    hbm = pl.BlockSpec(memory_space=pl.ANY)
    return pl.pallas_call(
        functools.partial(kernel, n),
        out_shape=jax.ShapeDtypeStruct((rows, width), BF16),
        in_specs=[vmem] * 4 + [hbm] * 2,
        out_specs=vmem,
        scratch_shapes=[
            pltpu.VMEM((width, units), BF16),
            pltpu.VMEM((units, width), BF16),
            pltpu.VMEM((n, CHUNKS, pair, wide), BF16),
            pltpu.VMEM((2, total, half), BF16),
            pltpu.VMEM((total, units), BF16),
            pltpu.VMEM((CHUNKS, total, wide), BF16),
            pltpu.VMEM((CHUNKS, total, wide), BF16),
            pltpu.VMEM((CHUNKS, total, wide), F32),
            pltpu.VMEM((2, far, CHUNKS, pair, wide), wire),
            pltpu.VMEM((2, far, CHUNKS, pair, wide), wire),
            pltpu.VMEM((2, 2, CHUNKS, pair, wide // 2), wire),
            pltpu.VMEM((2, 2, CHUNKS, pair, wide // 2), wire),
            pltpu.VMEM((CHUNKS, rows, wide), F32),
            dma((2,)),
            dma((2,)),
            dma((2, far, CHUNKS)),
            dma((2, far, CHUNKS)),
            dma((2, far + 1, CHUNKS)),
            dma((2, far + 1, CHUNKS)),
            dma((CHUNKS,)),
            dma((CHUNKS,)),
            dma((2, far, CHUNKS)),
            dma((2, far, CHUNKS)),
            dma((2, 2, CHUNKS)),
            dma((2, 2, CHUNKS)),
            dma((CHUNKS,)),
            dma((CHUNKS,)),
        ],
        compiler_params=pltpu.CompilerParams(
            collective_id=0, has_side_effects=True, vmem_limit_bytes=60 * 1024 * 1024
        ),
    )(tokens, norm_gain[None], b_expand[None], b_project[None], w_expand, w_project)


def solution(mesh):
    placed = (P(("groups", "blk"), None), P(), P(None, "blk"), P("blk"), P("blk", None), P())
    return jax.shard_map(
        functools.partial(on_device, mesh.shape["blk"]),
        mesh=mesh, in_specs=placed, out_specs=P(("groups", "blk"), None), check_vma=False,
    )
```

```python
import functools

import jax
import jax.numpy as jnp
from jax import lax
from jax.experimental import pallas as pl
from jax.experimental.pallas import tpu as pltpu
from jax.sharding import PartitionSpec as P

F32, BF16 = jnp.float32, jnp.bfloat16
CHUNKS = 4


def gelu_tanh(value):
    return 0.5 * value * (1.0 + jnp.tanh(0.7978845608 * (value + 0.044715 * value * value * value)))


def tile_of(size, most=768):
    step = 256 if size % 256 == 0 else 128
    return max(t for t in range(step, most + 1, step) if size % t == 0)


def chip_at(place, chips):
    if chips > 8:
        return place
    half = chips // 2
    down = lax.div(place, half)
    return (1 - down) * 2 * place + down * (2 * (chips - 1 - place) + 1)


def place_of(chip, chips):
    if chips > 8:
        return chip
    high, low = lax.div(chip, 2), lax.rem(chip, 2)
    return (1 - low) * high + low * (chips - 1 - high)


def kernel(
    n, tok, gain, b1, b2, w1, w2, out,
    w1v, w2v, xin, lhs, hid, snd, sib_in, own, ring_in, ring_out, last_in, last_out, ext_in,
    w1_sem, w2_sem, ag_send, ag_recv, fw_send, fw_recv, sib_send, sib_recv, rs_send, rs_recv, last_send, last_recv, ext_send, ext_recv,
):
    rows, width = tok.shape
    pair = 2 * rows
    chips = n // 2
    far = chips // 2
    half = width // 2
    wide = half // CHUNKS
    units = w1.shape[1]
    wire = ring_in.dtype
    ways = (0, 1)

    me = lax.axis_index("blk")
    core, chip = lax.rem(me, 2), lax.div(me, 2)
    place = place_of(chip, chips)

    def around(k):
        return chip_at(lax.rem(place + k + 2 * chips, chips), chips)

    sign = (1, -1)
    ahead = [around(sign[w]) * 2 + core for w in ways]
    beyond = [around(2 * sign[w]) * 2 + core for w in ways]
    across = [around(sign[w]) * 2 + 1 - core for w in ways]
    sibling = chip * 2 + 1 - core

    def takes(way, j):
        return (j % 2) == way

    def send(src, dst, send_sem, recv_sem, to):
        return pltpu.make_async_remote_copy(
            src_ref=src, dst_ref=dst, send_sem=send_sem, recv_sem=recv_sem,
            device_id={"blk": to}, device_id_type=pl.DeviceIdType.MESH,
        )

    barrier = pltpu.get_barrier_semaphore()
    for other in (*ahead, *across, *beyond, sibling):
        pl.semaphore_signal(barrier, inc=1, device_id={"blk": other}, device_id_type=pl.DeviceIdType.MESH)

    def w1_copy(h):
        at = pl.ds(h * half, half)
        return pltpu.make_async_copy(w1.at[at], w1v.at[at], w1_sem.at[h])

    def w2_copy(h):
        at = pl.ds(pl.multiple_of((core if h else 1 - core) * half, half), half)
        return pltpu.make_async_copy(w2.at[:, at], w2v.at[:, at], w2_sem.at[h])

    for h in ways:
        w1_copy(h).start()
    for h in ways:
        w2_copy(h).start()

    x = tok[...].astype(F32)
    mean = jnp.mean(x, axis=1, keepdims=True)
    centred = x - mean
    spread = jnp.mean(centred * centred, axis=1, keepdims=True)
    normed = centred / jnp.sqrt(spread + 1e-06) * gain[...]
    folded = jnp.concatenate([normed[:, :half], normed[:, half:]], axis=0).astype(BF16)
    for j in range(CHUNKS):
        xin[me, j] = folded[:, j * wide:(j + 1) * wide]

    pl.semaphore_wait(barrier, 7)

    def ag(way, s, j, where, leap=False):
        block = xin.at[where * 2 + core, j]
        return send(block, block, ag_send.at[way, s, j], ag_recv.at[way, s, j], (beyond if leap else ahead)[way])

    def fw(way, s, j, where, side):
        block = xin.at[where * 2 + side, j]
        return send(block, block, fw_send.at[way, s, j], fw_recv.at[way, s, j], sibling)

    def rows_of(where):
        return pl.ds(pl.multiple_of(where * pair, pair), pair)

    def assemble(where, chunks):
        for j in chunks:
            first, second = xin[where * 2, j].astype(F32), xin[where * 2 + 1, j].astype(F32)
            at = slice(j * wide, (j + 1) * wide)
            lhs[0, rows_of(where), at] = jnp.concatenate([first[:rows], second[:rows]], axis=0).astype(BF16)
            lhs[1, rows_of(where), at] = jnp.concatenate([first[rows:], second[rows:]], axis=0).astype(BF16)

    every = range(CHUNKS)
    for j in every:
        for way in ways:
            ag(way, 0, j, chip).start()
    for j in every:
        fw(0, 0, j, chip, core).start()

    def gather(s, onward, leap, last=False):
        for j in every:
            for way in ways:
                if last and not takes(way, j):
                    continue
                where = around(-sign[way] * s)
                ag(way, s - 1, j, where).wait_recv()
                if leap and takes(way, j):
                    ag(way, s + 1, j, where, True).start()
                if onward:
                    ag(way, s, j, where).start()
                fw(way, s, j, where, core).start()

    def take(s, last):
        for way in ways:
            where = around(-sign[way] * s)
            chunks = [j for j in every if not last or takes(way, j)]
            for j in chunks:
                fw(way, s, j, where, 1 - core).wait_recv()
            assemble(where, chunks)

    gather(1, True, False)
    for j in every:
        fw(0, 0, j, chip, 1 - core).wait_recv()
    assemble(chip, every)

    @pl.loop(2, far - 2)
    def _(s):
        gather(s, True, False)
        take(s - 1, False)

    gather(far - 2, True, True)
    take(far - 3, False)
    gather(far - 1, False, False)
    gather(far, False, False, True)
    take(far - 2, False)
    take(far - 1, False)
    take(far, True)

    for h in ways:
        w1_copy(h).wait()

    tile = tile_of(units)

    @pl.loop(0, units // tile)
    def _(t):
        at = pl.ds(pl.multiple_of(t * tile, tile), tile)
        total = jnp.dot(lhs[0], w1v[:half, at], preferred_element_type=F32)
        total += jnp.dot(lhs[1], w1v[half:, at], preferred_element_type=F32)
        bias = [b1[pl.ds(t * (tile // 128) + i, 1), :] for i in range(tile // 128)]
        hid[:, at] = gelu_tanh(total + jnp.concatenate(bias, axis=1)).astype(BF16)

    cut = tile_of(wide)

    def project(side, j, store):
        @pl.loop(0, wide // cut)
        def _(t):
            at = pl.ds(pl.multiple_of(t * cut, cut), cut)
            cols = pl.ds(pl.multiple_of(side * half + j * wide + t * cut, cut), cut)
            store(at, jnp.dot(hid[...], w2v[:, cols], preferred_element_type=F32))

    def sib_copy(j):
        return send(snd.at[j], sib_in.at[j], sib_send.at[j], sib_recv.at[j], sibling)

    w2_copy(0).wait()
    for j in every:

        def keep_theirs(at, value, j=j):
            snd[j, :, at] = value.astype(BF16)

        project(1 - core, j, keep_theirs)
        sib_copy(j).start()

    def rs(way, k, j, leap=False):
        return send(
            ring_out.at[way, k - 1, j], ring_in.at[way, k - 1, j],
            rs_send.at[way, k - 1, j], rs_recv.at[way, k - 1, j], (beyond if leap else ahead)[way],
        )

    def ours(j, where):
        return own[j, rows_of(where), :] + sib_in[j, rows_of(where), :].astype(F32)

    def came(way, k, j):
        rs(way, k, j).wait_recv()
        return ring_in[way, k - 1, j].astype(F32)

    def running(way, k, j):
        total = ours(j, around(sign[way] * k))
        if isinstance(k, int) and k >= far - 1:
            return total
        total += came(way, k + 1, j)
        if isinstance(k, int) and k == far - 2 and takes(way, j):
            total += came(way, k + 2, j)
        return total

    def pass_on(way, k, j, leap=False):
        ring_out[way, k - 1, j] = running(way, k, j).astype(wire)
        rs(way, k, j, leap).start()

    def last_copy(way, j, side):
        to = around(sign[way]) * 2 + side
        return send(
            last_out.at[way, side, j], last_in.at[way, core, j],
            last_send.at[way, side, j], last_recv.at[way, core, j], to,
        )

    def last_came(way, j, side):
        return send(
            last_out.at[way, 0, j], last_in.at[way, side, j],
            last_send.at[way, 0, j], last_recv.at[way, side, j], sibling,
        )

    def fold(value):
        return jnp.concatenate([value[:, :wide // 2], value[:, wide // 2:]], axis=0)

    def unfold(value):
        return jnp.concatenate([value[:rows], value[rows:]], axis=1)

    def ext_copy(j):
        theirs = pl.ds(pl.multiple_of(chip * pair + (1 - core) * rows, rows), rows)
        return send(own.at[j, theirs], ext_in.at[j], ext_send.at[j], ext_recv.at[j], sibling)

    w2_copy(1).wait()
    for j in every:

        def keep_own(at, value, j=j):
            own[j, :, at] = value

        project(core, j, keep_own)
        sib_copy(j).wait_recv()
        for way in ways:
            if takes(way, j):
                pass_on(way, far, j, True)
        for way in ways:
            pass_on(way, far - 1, j)
        ext_copy(j).start()

    if far > 3:
        for j in every:
            for way in ways:
                pass_on(way, far - 2, j)

    @pl.loop(3, far - 1)
    def _(s):
        for j in every:
            for way in ways:
                pass_on(way, far - s, j)

    for j in every:
        for way in ways:
            total = running(way, 1, j)
            for side in (0, 1):
                last_out[way, side, j] = fold(total[side * rows:(side + 1) * rows]).astype(wire)
                last_copy(way, j, side).start()

    def my_rows(value):
        return jnp.where(core == 0, value[:rows], value[rows:])

    for j in every:
        ext_copy(j).wait_recv()
        mine = own[j, pl.ds(pl.multiple_of(chip * pair + core * rows, rows), rows), :]
        mine += my_rows(sib_in[j, rows_of(chip), :].astype(F32))
        other = my_rows(snd[j, rows_of(chip), :].astype(F32)) + ext_in[j]
        for side in (0, 1):
            start = side * half + j * wide
            at = slice(start, start + wide)
            total = jnp.where(core == side, mine, other) + b2[:, at]
            for way in ways:
                last_came(way, j, side).wait_recv()
                total += unfold(last_in[way, side, j].astype(F32))
            out[:, at] = total.astype(BF16)

    def sent(s, last):
        for j in every:
            for way in ways:
                if not last or takes(way, j):
                    ag(way, s - 1, j, chip).wait_send()
                    fw(way, s, j, chip, core).wait_send()

    def scattered(k, last):
        for j in every:
            for way in ways:
                if not last or takes(way, j):
                    rs(way, k, j).wait_send()

    for j in every:
        fw(0, 0, j, chip, core).wait_send()
        sib_copy(j).wait_send()
        ext_copy(j).wait_send()
        for way in ways:
            for side in (0, 1):
                last_copy(way, j, side).wait_send()

    @pl.loop(1, far)
    def _(s):
        sent(s, False)

    @pl.loop(2, far)
    def _(k):
        scattered(k, False)

    sent(far, True)
    scattered(far, True)


def on_device(n, tokens, norm_gain, w_expand, b_expand, w_project, b_project):
    rows, width = tokens.shape
    units = w_expand.shape[1]
    chips = n // 2
    far = chips // 2
    pair, total = 2 * rows, rows * n
    half = width // 2
    wide = half // CHUNKS
    wire = BF16 if chips <= 8 else F32
    dma = pltpu.SemaphoreType.DMA
    vmem = pl.BlockSpec(memory_space=pltpu.VMEM)
    hbm = pl.BlockSpec(memory_space=pl.ANY)
    return pl.pallas_call(
        functools.partial(kernel, n),
        out_shape=jax.ShapeDtypeStruct((rows, width), BF16),
        in_specs=[vmem] * 4 + [hbm] * 2,
        out_specs=vmem,
        scratch_shapes=[
            pltpu.VMEM((width, units), BF16),
            pltpu.VMEM((units, width), BF16),
            pltpu.VMEM((n, CHUNKS, pair, wide), BF16),
            pltpu.VMEM((2, total, half), BF16),
            pltpu.VMEM((total, units), BF16),
            pltpu.VMEM((CHUNKS, total, wide), BF16),
            pltpu.VMEM((CHUNKS, total, wide), BF16),
            pltpu.VMEM((CHUNKS, total, wide), F32),
            pltpu.VMEM((2, far, CHUNKS, pair, wide), wire),
            pltpu.VMEM((2, far, CHUNKS, pair, wide), wire),
            pltpu.VMEM((2, 2, CHUNKS, pair, wide // 2), wire),
            pltpu.VMEM((2, 2, CHUNKS, pair, wide // 2), wire),
            pltpu.VMEM((CHUNKS, rows, wide), F32),
            dma((2,)),
            dma((2,)),
            dma((2, far, CHUNKS)),
            dma((2, far, CHUNKS)),
            dma((2, far + 1, CHUNKS)),
            dma((2, far + 1, CHUNKS)),
            dma((CHUNKS,)),
            dma((CHUNKS,)),
            dma((2, far, CHUNKS)),
            dma((2, far, CHUNKS)),
            dma((2, 2, CHUNKS)),
            dma((2, 2, CHUNKS)),
            dma((CHUNKS,)),
            dma((CHUNKS,)),
        ],
        compiler_params=pltpu.CompilerParams(
            collective_id=0, has_side_effects=True, vmem_limit_bytes=60 * 1024 * 1024
        ),
    )(tokens, norm_gain[None], b_expand.reshape(units // 128, 128), b_project[None], w_expand, w_project)


def solution(mesh):
    placed = (P(("groups", "blk"), None), P(), P(None, "blk"), P("blk"), P("blk", None), P())
    return jax.shard_map(
        functools.partial(on_device, mesh.shape["blk"]),
        mesh=mesh, in_specs=placed, out_specs=P(("groups", "blk"), None), check_vma=False,
    )
```
